32 devices in a mesh: expert: 8 (over z, y), shard: 4 (over x, core).
Axes of the slice: x: 2, y: 2, z: 4, core: 2. Of those that a mesh axis runs over, the one named last changes fastest.
Arguments:
- layer_input: bfloat16 [8192, 768], P(('expert', 'shard')), may hold values from -6 to 6
- norm_gain: float32 [768], replicated, may hold values from 0.1 to 1.9
- query_weight: bfloat16 [768, 768], P(None, 'shard'), may hold values from -0.21875 to 0.21875
- key_weight: bfloat16 [768, 768], P(None, 'shard'), may hold values from -0.21875 to 0.21875
- value_weight: bfloat16 [768, 768], P(None, 'shard'), may hold values from -0.21875 to 0.21875
- output_weight: bfloat16 [768, 768], P('shard'), may hold values from -1.75 to 1.75
- bias_table: float32 [32, 12], P(None, 'shard'), may hold values from -3 to 3
- mixing_gain: float32 [768], replicated, may hold values from 0.1 to 1.9
- router_weight: float32 [768, 8], replicated, may hold values from -0.15625 to 0.15625
- up_weight: bfloat16 [8, 768, 3072], P('expert', None, 'shard'), may hold values from -0.21875 to 0.21875
- down_weight: bfloat16 [8, 3072, 768], P('expert', 'shard'), may hold values from -0.109375 to 0.109375
- expert_routes: int32 [8192, 2], P(('expert', 'shard')), may hold values from 0 to 7, all different within a row; in each aligned block of 256 rows (0 to 255, 256 to 511, ...) at most 128 rows name the same one
- cotangent: bfloat16 [8192, 768], P(('expert', 'shard')), may hold values from -6 to 6
Outputs:
- layer_output: bfloat16 [8192, 768], P(('expert', 'shard'))
- input_grad: bfloat16 [8192, 768], P(('expert', 'shard'))
- gain_grad: float32 [768], replicated
- query_grad: float32 [768, 768], P(None, 'shard')
- key_grad: float32 [768, 768], P(None, 'shard')
- value_grad: float32 [768, 768], P(None, 'shard')
- output_grad: float32 [768, 768], P('shard')
- table_grad: float32 [32, 12], P(None, 'shard')
- mixing_grad: float32 [768], replicated
- router_grad: float32 [768, 8], replicated
- up_grad: float32 [8, 768, 3072], P('expert', None, 'shard')
- down_grad: float32 [8, 3072, 768], P('expert', 'shard')
The draws below stay inside these ranges and needn't reach their ends.
Inputs may be any that keep to these rules, and one draw needn't show every extreme that they name: `expert_routes`: each row names two different experts. Among the 256 rows of one device no expert is named by more than 128 rows, and in every draw some device has an expert named by exactly 128 of its rows.
All inputs are finite; a program needn't handle non-finite values.
Results may differ from the reference program's by a relative error of at most 0.015.
Values may be sent and summed in bfloat16 or wider, within the bound.
A program may use at most 192 MiB of HBM per device.

```python
import math
import jax
import jax.numpy as jnp
import numpy as np
from jax import lax

D = 768
HEADS = 12
HEAD_DIM = 64
FF = 3072
BUCKETS = 32
MAX_DIST = 128
SEQ = 1024
EXPERTS = 8
ROWS = 256
CAP = 128
TOKENS = 8192


def steps_of(stream_key, extent, shards, low, high):
    factor_of, own = 1.0, jax.random.fold_in(stream_key, 6)
    for dim, blocks in shards:
        draws = jnp.exp(jax.random.uniform(jax.random.fold_in(own, dim), (blocks,), jnp.float32, low / len(shards), high / len(shards)))
        factor_of = factor_of * jnp.repeat(draws, extent[dim] // blocks).reshape([-1 if axis == dim else 1 for axis in range(len(extent))])
    return factor_of


def routed_block(own_key, own, number, rows, number_of, top, limit, lean):
    order = jax.random.permutation(own_key, number_of)
    crowded, ordinary = shares(number_of, rows * top, limit, lean, True), shares(number_of, rows * top, limit, lean, False)
    places = jnp.arange(number_of)

    def named(sizes, turn):
        used = int((sizes > 0).sum())
        fixed = max(1, used // 4)
        moved = fixed + (places - fixed + turn * (used - fixed)) % max(1, number_of - fixed)
        return jnp.zeros((number_of,), jnp.int32).at[order[jnp.where(places < fixed, places, moved)]].set(jnp.asarray(sizes, jnp.int32))

    sizes = jnp.where(number % 4 == 0, named(crowded, number // 4), named(ordinary, number - number // 4 - 1))
    mixed = jax.random.permutation(jax.random.fold_in(own, 3), number_of)
    giver, sink = mixed[0:number_of // 2 * 2:2], mixed[1:number_of // 2 * 2:2]
    slack = jnp.minimum(sizes[giver] - 1, limit - sizes[sink]) // 2
    slack = jnp.where((giver == order[0]) | (sink == order[0]) | (sizes[sink] == 0), 0, jnp.maximum(slack, 0))
    moved = jax.random.randint(jax.random.fold_in(own, 4), (number_of // 2,), 0, 1 << 20) % (slack + 1)
    sizes = sizes.at[giver].add(-moved).at[sink].add(moved)
    items = jnp.searchsorted(jnp.cumsum(sizes), jnp.arange(rows * top), side="right").astype(jnp.int32)
    table = items.reshape(top, rows).T
    table = table[jax.random.permutation(jax.random.fold_in(own, 1), rows)]
    turn = jax.random.randint(jax.random.fold_in(own, 2), (rows, 1), 0, top)
    return jnp.take_along_axis(table, (jnp.arange(top)[None, :] + turn) % top, axis=1)


def shares(amount, total, reach, slope, full):
    portions = [(1 << 20) // math.isqrt(standing ** slope) + 1 for standing in range(1, amount + 1)]
    largest = reach if full else min(reach, max(-(-total // amount), total * portions[0] // sum(portions)))
    least = 1 if total - largest >= amount - 1 else 0
    counts, surplus = [largest] + [least] * (amount - 1), total - largest - least * (amount - 1)
    while surplus > 0:
        movable = [i for i in range(1, amount) if counts[i] < largest] or [i for i in range(1, amount) if counts[i] < reach]
        whole, remaining = sum([portions[i] for i in movable]), surplus
        for i in movable:
            addition = min(reach - counts[i], max(1, remaining * portions[i] // whole), surplus)
            counts[i] = counts[i] + addition
            surplus = surplus - addition
    return np.array(counts)


def gaussian(own_key, shape, deviation, limit, split=(), kind=jnp.bfloat16):
    loudness = steps_of(own_key, shape, split, -0.22, 0.18) if split else 1.0
    array = jax.random.normal(own_key, shape, jnp.float32) * deviation * loudness
    return jnp.minimum(jnp.maximum(array, -limit), limit).astype(kind)


def setup_inputs(seed: int = 0) -> dict:
    arg_keys = jax.random.split(jax.random.key(seed), 14)
    layer_input = gaussian(arg_keys[0], (TOKENS, D), 1.0, 6.0, ((0, 32),))
    norm_gain = jnp.clip(1.0 + 0.18 * jax.random.normal(arg_keys[1], (D,), jnp.float32), 0.1, 1.9)
    query_weight = gaussian(arg_keys[2], (D, HEADS * HEAD_DIM), D ** -0.5, 0.21875, ((1, 4),))
    key_weight = gaussian(arg_keys[3], (D, HEADS * HEAD_DIM), D ** -0.5, 0.21875, ((1, 4),))
    value_weight = gaussian(arg_keys[4], (D, HEADS * HEAD_DIM), D ** -0.5, 0.21875, ((1, 4),))
    output_weight = gaussian(arg_keys[5], (HEADS * HEAD_DIM, D), (max(1, D // 64)) ** -0.5, 1.75, ((0, 4),))
    bias_table = gaussian(arg_keys[6], (BUCKETS, HEADS), 0.5, 3.0, ((1, 4),), jnp.float32)
    mixing_gain = jnp.clip(1.0 + 0.18 * jax.random.normal(arg_keys[7], (D,), jnp.float32), 0.1, 1.9)
    router_weight = gaussian(arg_keys[8], (D, EXPERTS), (2 * D) ** -0.5, 0.15625, (), jnp.float32)
    up_weight = gaussian(arg_keys[9], (EXPERTS, D, FF), D ** -0.5, 0.21875, ((0, 8), (2, 4)))
    down_weight = gaussian(arg_keys[10], (EXPERTS, FF, D), FF ** -0.5, 0.109375, ((0, 8), (1, 4)))
    expert_routes_keys = jax.random.split(jax.random.fold_in(arg_keys[11], 1), TOKENS // ROWS)
    expert_routes_turns = jax.random.permutation(jax.random.fold_in(arg_keys[11], 3), TOKENS // ROWS)
    expert_routes = jax.vmap(lambda own, number: routed_block(jax.random.fold_in(arg_keys[11], 2), own, number, ROWS, EXPERTS, 2, CAP, 1))(expert_routes_keys, expert_routes_turns).reshape((TOKENS, 2))
    cotangent = gaussian(arg_keys[12], (TOKENS, D), 1.0, 6.0, ((0, 32),))
    return dict(layer_input=layer_input, norm_gain=norm_gain, query_weight=query_weight, key_weight=key_weight, value_weight=value_weight, output_weight=output_weight, bias_table=bias_table, mixing_gain=mixing_gain, router_weight=router_weight, up_weight=up_weight, down_weight=down_weight, expert_routes=expert_routes, cotangent=cotangent)


@jax.custom_vjp
def low(v):
    return lax.optimization_barrier(v.astype(jnp.bfloat16)).astype(jnp.float32)

@jax.custom_vjp
def lower_precision_backward(v):
    return v

def low_keep(v):
    return (low(v), None)

def low_pass(kept, grad):
    return (grad,)

def back_keep(v):
    return (v, None)

def back_low(kept, grad):
    return (low(grad),)
low.defvjp(low_keep, low_pass)
lower_precision_backward.defvjp(back_keep, back_low)

def matmul(left, right):
    return jnp.dot(left, right, precision=lax.Precision.HIGHEST, preferred_element_type=jnp.float32)

def rms_scale(values, gain):
    return values * lax.rsqrt(lax.optimization_barrier(jnp.mean(values * values, axis=-1, keepdims=True)) + 1e-06) * gain

def gelu_tanh(values):
    return jax.nn.gelu(values, approximate=True)

def bucket_ids(distance):
    halfway = BUCKETS // 2
    far_bucket = jnp.full_like(distance, halfway)
    for bucket in range(halfway + 1, BUCKETS):
        threshold = int(math.ceil(halfway * (MAX_DIST / halfway) ** ((bucket - halfway) / halfway)))
        far_bucket = far_bucket + (distance >= threshold).astype(jnp.int32)
    return jnp.where(distance < halfway, distance, far_bucket)

def bias_rows(table_values, row_start, span, length):
    distance = jnp.arange(length, dtype=jnp.int32)
    onehot = (bucket_ids(distance)[:, None] == jnp.arange(BUCKETS, dtype=jnp.int32)[None, :]).astype(jnp.float32)
    per_distance = jnp.dot(onehot, table_values, precision=lax.Precision.HIGHEST, preferred_element_type=jnp.float32).T
    head_count = per_distance.shape[0]
    extended = jnp.concatenate([jnp.zeros((head_count, length - 1), jnp.float32), per_distance], axis=1)
    window = lax.dynamic_slice_in_dim(extended, row_start, span + length - 1, 1)
    flipped = window[:, ::-1]
    stride = span + length
    repeated = jnp.tile(flipped, (1, span + 1))[:, :span * stride]
    return repeated.reshape(head_count, span, stride)[:, ::-1, :length]

def attend_sequence(packed, table_values):
    queries, key_rows, value_rows = packed
    scale = HEAD_DIM ** (-0.5)
    span = min(512, SEQ)
    query_heads = queries.reshape(SEQ, HEADS, HEAD_DIM)
    key_heads = key_rows.reshape(SEQ, HEADS, HEAD_DIM)
    value_heads = value_rows.reshape(SEQ, HEADS, HEAD_DIM)

    def block_rows(row_start):
        query_block = lax.dynamic_slice_in_dim(query_heads, row_start, span, 0)
        scores = jnp.einsum('ahd,jhd->haj', query_block, key_heads, precision=lax.Precision.HIGHEST) * scale
        scores = lower_precision_backward(scores + bias_rows(table_values, row_start, span, SEQ))
        position = row_start + jnp.arange(span, dtype=jnp.int32)
        causal = position[:, None] >= jnp.arange(SEQ, dtype=jnp.int32)[None, :]
        scores = jnp.where(causal[None], scores, -1e+30)
        weights = low(jax.nn.softmax(scores, axis=-1))
        result = jnp.einsum('haj,jhd->ahd', weights, value_heads, precision=lax.Precision.HIGHEST)
        return result.reshape(span, HEADS * HEAD_DIM)
    starts = jnp.arange(SEQ // span, dtype=jnp.int32) * span
    return lax.map(jax.checkpoint(block_rows), starts).reshape(SEQ, HEADS * HEAD_DIM)

def slot_tables(expert_routes):
    block_count = TOKENS // ROWS
    flat_routes = expert_routes.reshape(block_count, 2 * ROWS)
    onehot = (flat_routes[:, :, None] == jnp.arange(EXPERTS, dtype=jnp.int32)).astype(jnp.int32)
    slots = lax.optimization_barrier(jnp.sum(jnp.cumsum(onehot, axis=1) * onehot, axis=-1)) - 1
    position = jnp.arange(block_count, dtype=jnp.int32)[:, None] * CAP + slots
    assignment = jnp.arange(block_count * 2 * ROWS, dtype=jnp.int32).reshape(block_count, 2 * ROWS)
    slot_owner = jnp.full((EXPERTS, block_count * CAP), -1, jnp.int32)
    return slot_owner.at[flat_routes, position].set(assignment)

def forward(layer_input, norm_gain, query_weight, key_weight, value_weight, output_weight, bias_table, mixing_gain, router_weight, up_weight, down_weight, slot_owner, expert_routes):
    normed = low(rms_scale(layer_input, norm_gain))
    queries = low(lower_precision_backward(matmul(normed, query_weight)))
    key_rows = low(lower_precision_backward(matmul(normed, key_weight)))
    value_rows = low(lower_precision_backward(matmul(normed, value_weight)))
    seq_count = TOKENS // SEQ
    stacked = (queries.reshape(seq_count, SEQ, -1), key_rows.reshape(seq_count, SEQ, -1), value_rows.reshape(seq_count, SEQ, -1))
    attended = lax.map(lambda packed: attend_sequence(packed, bias_table), stacked)
    attended = low(lower_precision_backward(attended.reshape(TOKENS, HEADS * HEAD_DIM)))
    branch = lower_precision_backward(matmul(attended, output_weight))
    residual = layer_input + branch
    mixed = rms_scale(residual, mixing_gain)
    logits = matmul(mixed, router_weight)
    chosen = jnp.take_along_axis(logits, expert_routes, axis=1)
    gate_probs = jax.nn.softmax(chosen, axis=-1)
    flattened_gate_values = gate_probs.reshape(-1)
    dispatched_rows = low(mixed)
    live_slots = slot_owner >= 0
    owner_index = jnp.maximum(slot_owner, 0)
    token_index = owner_index // 2

    def expert_step(accumulated, packed):
        up_matrix, down_matrix, token_row_block, assigned_row_list, active_rows = packed
        active_mask = active_rows.astype(jnp.float32)[:, None]
        incoming_rows = lower_precision_backward(dispatched_rows[token_row_block] * active_mask)
        hidden = lower_precision_backward(matmul(incoming_rows, up_matrix))
        activated = low(gelu_tanh(hidden))
        returned_rows = low(lower_precision_backward(matmul(activated, down_matrix)))
        gate_weighted_rows = returned_rows * (flattened_gate_values[assigned_row_list][:, None] * active_mask)
        return (accumulated.at[token_row_block].add(gate_weighted_rows), None)
    mixture, unused = lax.scan(jax.checkpoint(expert_step), jnp.zeros_like(residual), (up_weight, down_weight, token_index, owner_index, live_slots))
    return residual + mixture

def reference(layer_input, norm_gain, query_weight, key_weight, value_weight, output_weight, bias_table, mixing_gain, router_weight, up_weight, down_weight, expert_routes, cotangent):
    slot_owner = slot_tables(expert_routes)
    floats = (layer_input.astype(jnp.float32), norm_gain, query_weight.astype(jnp.float32), key_weight.astype(jnp.float32), value_weight.astype(jnp.float32), output_weight.astype(jnp.float32), bias_table, mixing_gain, router_weight, up_weight.astype(jnp.float32), down_weight.astype(jnp.float32))
    result, pullback = jax.vjp(lambda *params: forward(*params, slot_owner, expert_routes), *floats)
    grads = pullback(cotangent.astype(jnp.float32))
    return (result.astype(jnp.bfloat16), grads[0].astype(jnp.bfloat16), grads[1], grads[2], grads[3], grads[4], grads[5], grads[6], grads[7], grads[8], grads[9], grads[10])
```

```python
import math

import jax
import jax.numpy as jnp
from jax import lax
from jax.experimental import pallas as pl
from jax.experimental.pallas import tpu as pltpu
from jax.sharding import PartitionSpec as P

HEAD_DIM = 64
BUCKETS = 32
MAX_DIST = 128
TILE = 128
SPAN = 256
SCALE = HEAD_DIM ** (-0.5)
VMEM_BYTES = 56 * 1024 * 1024
F32 = jnp.float32
BF16 = jnp.bfloat16


def thresholds():
    halfway = BUCKETS // 2
    values = list(range(halfway + 1))
    for bucket in range(halfway + 1, BUCKETS):
        values.append(
            int(math.ceil(halfway * (MAX_DIST / halfway) ** ((bucket - halfway) / halfway)))
        )
    return values


STARTS = thresholds()


def nn(a, b):
    return lax.dot_general(a, b, (((1,), (0,)), ((), ())), preferred_element_type=F32)


def nt(a, b):
    return lax.dot_general(a, b, (((1,), (1,)), ((), ())), preferred_element_type=F32)


def tn(a, b):
    return lax.dot_general(a, b, (((0,), (0,)), ((), ())), preferred_element_type=F32)


def tile_distance():
    key = lax.broadcasted_iota(jnp.int32, (TILE, TILE), 0)
    query = lax.broadcasted_iota(jnp.int32, (TILE, TILE), 1)
    return query - key


def bias_tiles(table_ref, head):
    near = tile_distance()

    def chain(distance):
        value = jnp.full((TILE, TILE), table_ref[0, head], F32)
        for bucket in range(1, BUCKETS):
            value = jnp.where(distance >= STARTS[bucket], table_ref[bucket, head], value)
        return value

    diagonal = jnp.where(near >= 0, chain(near), -1e30)
    beside = chain(near + TILE)
    far = jnp.full((TILE, TILE), table_ref[BUCKETS - 1, head], F32)
    masked = jnp.full((TILE, TILE), -1e30, F32)
    return diagonal, beside, far, masked


def pick_tile(tiles, offset):
    if offset < 0:
        return tiles[3]
    return tiles[min(offset, 2)]


def bias_block(tiles, block):
    per = SPAN // TILE
    strips = []
    for key_tile in range(per * (block + 1)):
        strips.append(
            jnp.concatenate(
                [pick_tile(tiles, per * block + part - key_tile) for part in range(per)], axis=1
            )
        )
    return jnp.concatenate(strips, axis=0)


def attend_kernel(
    table_ref, x_ref, gain_ref, qkv_weight_ref, out_weight_ref,
    branch_ref, normed_ref, q_ref, k_ref, v_ref, att_ref, lse_ref,
):
    length = x_ref.shape[0]
    heads = q_ref.shape[0]
    local = heads * HEAD_DIM
    for block in range(length // SPAN):
        rows = slice(block * SPAN, (block + 1) * SPAN)
        x = x_ref[rows, :].astype(F32)
        norm_scale = lax.rsqrt(jnp.mean(x * x, axis=-1, keepdims=True) + 1e-06)
        normed = (x * norm_scale * gain_ref[...]).astype(BF16)
        normed_ref[rows, :] = normed
        qkv = nn(normed, qkv_weight_ref[...])
        for head in range(heads):
            cols = head * HEAD_DIM
            query = qkv[:, cols : cols + HEAD_DIM].astype(BF16)
            q_ref[head, rows, :] = (query.astype(F32) * SCALE).astype(BF16)
            k_ref[head, rows, :] = qkv[:, local + cols : local + cols + HEAD_DIM].astype(BF16)
            v_ref[head, rows, :] = qkv[:, 2 * local + cols : 2 * local + cols + HEAD_DIM].astype(
                BF16
            )
    lse_ref[...] = jnp.zeros_like(lse_ref)
    for head in range(heads):
        tiles = bias_tiles(table_ref, head)
        values_t = v_ref[head].astype(F32).T.astype(BF16)
        for block in range(length // SPAN):
            rows = slice(block * SPAN, (block + 1) * SPAN)
            reach = (block + 1) * SPAN
            scores = nt(k_ref[head, :reach, :], q_ref[head, rows, :]) + bias_block(tiles, block)
            maximum = jnp.max(scores, axis=0, keepdims=True)
            expo = jnp.exp(scores - maximum)
            totals = jnp.sum(expo, axis=0, keepdims=True)
            out_t = nn(values_t[:, :reach], expo.astype(BF16)) / totals
            att_ref[rows, head * HEAD_DIM : (head + 1) * HEAD_DIM] = out_t.T.astype(BF16)
            lse_ref[head : head + 1, rows] = maximum + jnp.log(totals)
    for block in range(length // SPAN):
        rows = slice(block * SPAN, (block + 1) * SPAN)
        branch_ref[rows, :] = nn(att_ref[rows, :], out_weight_ref[...]).astype(BF16)


def vmem_spec():
    return pl.BlockSpec(memory_space=pltpu.VMEM)


def attend(table, x_full, gain, qkv_weight, out_weight):
    length, width = x_full.shape
    local = out_weight.shape[0]
    heads = local // HEAD_DIM
    head_shape = jax.ShapeDtypeStruct((heads, length, HEAD_DIM), BF16)
    return pl.pallas_call(
        attend_kernel,
        out_shape=(
            jax.ShapeDtypeStruct((length, width), BF16),
            jax.ShapeDtypeStruct((length, width), BF16),
            head_shape,
            head_shape,
            head_shape,
            jax.ShapeDtypeStruct((length, local), BF16),
            jax.ShapeDtypeStruct((8, length), F32),
        ),
        in_specs=[pl.BlockSpec(memory_space=pltpu.SMEM)] + [vmem_spec()] * 4,
        out_specs=(vmem_spec(),) * 7,
        compiler_params=pltpu.CompilerParams(vmem_limit_bytes=VMEM_BYTES),
        cost_estimate=pl.CostEstimate(
            flops=12 * 10**9, bytes_accessed=8 * 10**6, transcendentals=2 * 10**6
        ),
        name="attend",
    )(table, x_full, gain.reshape(1, width), qkv_weight, out_weight)


def attend_back_kernel(
    table_ref, x_ref, qkv_weight_ref, out_weight_ref, q_ref, k_ref, v_ref, lse_ref, delta_ref,
    parts_ref, total_ref, gain_ref, table_grad_ref,
    att_delta_ref, key_ref, value_ref,
):
    length = x_ref.shape[0]
    heads = q_ref.shape[0]
    local = heads * HEAD_DIM
    blocks = length // SPAN
    per = SPAN // TILE
    near = tile_distance()
    for block in range(blocks):
        rows = slice(block * SPAN, (block + 1) * SPAN)
        att_delta = nt(delta_ref[rows, :], out_weight_ref[...])
        for head in range(heads):
            att_delta_ref[head, rows, :] = att_delta[
                :, head * HEAD_DIM : (head + 1) * HEAD_DIM
            ].astype(BF16)
    for head in range(heads):
        tiles = bias_tiles(table_ref, head)
        keys_t = k_ref[head].astype(F32).T.astype(BF16)
        sum_near = jnp.zeros((TILE, TILE), F32)
        sum_next = jnp.zeros((TILE, TILE), F32)
        sum_far = jnp.zeros((1, SPAN), F32)
        key_ref[...] = jnp.zeros_like(key_ref)
        value_ref[...] = jnp.zeros_like(value_ref)
        for block in range(blocks):
            rows = slice(block * SPAN, (block + 1) * SPAN)
            reach = (block + 1) * SPAN
            query = q_ref[head, rows, :]
            delta = att_delta_ref[head, rows, :]
            scores = nt(k_ref[head, :reach, :], query) + bias_block(tiles, block)
            weights = jnp.exp(scores - lse_ref[head : head + 1, rows])
            weight_delta = nt(v_ref[head, :reach, :], delta)
            centre = jnp.sum(weights * weight_delta, axis=0, keepdims=True)
            score_delta = (weights * (weight_delta - centre)).astype(BF16)
            value_ref[:reach, :] += nn(weights.astype(BF16), delta)
            key_ref[:reach, :] += nn(score_delta, query)
            query_t = nn(keys_t[:, :reach], score_delta) * SCALE
            parts_ref[rows, head * HEAD_DIM : (head + 1) * HEAD_DIM] = query_t.T.astype(BF16)
            rounded = score_delta.astype(F32)
            far_keys = max(0, (per * block - 1) * TILE)
            if far_keys:
                sum_far = sum_far + jnp.sum(rounded[:far_keys, :], axis=0, keepdims=True)
            for key_tile in range(far_keys // TILE, per * (block + 1)):
                for part in range(per):
                    offset = per * block + part - key_tile
                    if offset < 0:
                        continue
                    piece = rounded[
                        key_tile * TILE : (key_tile + 1) * TILE, part * TILE : (part + 1) * TILE
                    ]
                    if offset == 0:
                        sum_near = sum_near + piece
                    elif offset == 1:
                        sum_next = sum_next + piece
                    else:
                        total = jnp.sum(piece, axis=0, keepdims=True)
                        sum_far = sum_far + jnp.concatenate(
                            [total, jnp.zeros((1, SPAN - TILE), F32)], axis=1
                        )
        base = local + head * HEAD_DIM
        parts_ref[:, base : base + HEAD_DIM] = key_ref[...].astype(BF16)
        base = 2 * local + head * HEAD_DIM
        parts_ref[:, base : base + HEAD_DIM] = value_ref[...].astype(BF16)
        lines = []
        for bucket in range(BUCKETS):
            line = jnp.zeros((1, TILE), F32)
            for distance, sums in ((near, sum_near), (near + TILE, sum_next)):
                inside = distance >= STARTS[bucket]
                if bucket + 1 < BUCKETS:
                    inside = inside & (distance < STARTS[bucket + 1])
                line = line + jnp.sum(jnp.where(inside, sums, 0.0), axis=0, keepdims=True)
            if bucket == BUCKETS - 1:
                line = line + sum_far[:, :TILE] + sum_far[:, TILE:]
            lines.append(line)
        table_grad_ref[:, head : head + 1] = jnp.sum(
            jnp.concatenate(lines, axis=0), axis=1, keepdims=True
        )
    gain = jnp.zeros((1, x_ref.shape[1]), F32)
    for block in range(blocks):
        rows = slice(block * SPAN, (block + 1) * SPAN)
        total = nt(parts_ref[rows, :], qkv_weight_ref[...])
        x = x_ref[rows, :].astype(F32)
        norm_scale = lax.rsqrt(jnp.mean(x * x, axis=-1, keepdims=True) + 1e-06)
        gain = gain + jnp.sum(total * x * norm_scale, axis=0, keepdims=True)
        total_ref[rows, :] = total.astype(BF16)
    gain_ref[...] = gain


def attend_back(table, x_full, qkv_weight, out_weight, q, k, v, lse, delta):
    length, width = x_full.shape
    local = out_weight.shape[0]
    heads = local // HEAD_DIM
    return pl.pallas_call(
        attend_back_kernel,
        out_shape=(
            jax.ShapeDtypeStruct((length, 3 * local), BF16),
            jax.ShapeDtypeStruct((length, width), BF16),
            jax.ShapeDtypeStruct((1, width), F32),
            jax.ShapeDtypeStruct((BUCKETS, heads), F32),
        ),
        in_specs=[pl.BlockSpec(memory_space=pltpu.SMEM)] + [vmem_spec()] * 8,
        out_specs=(vmem_spec(),) * 4,
        scratch_shapes=[
            pltpu.VMEM((heads, length, HEAD_DIM), BF16),
            pltpu.VMEM((length, HEAD_DIM), F32),
            pltpu.VMEM((length, HEAD_DIM), F32),
        ],
        compiler_params=pltpu.CompilerParams(vmem_limit_bytes=VMEM_BYTES),
        cost_estimate=pl.CostEstimate(
            flops=24 * 10**9, bytes_accessed=12 * 10**6, transcendentals=2 * 10**6
        ),
        name="attend_back",
    )(table, x_full, qkv_weight, out_weight, q, k, v, lse, delta)


def experts_kernel(
    rows_ref, delta_ref, up_ref, down_ref,
    out_ref, row_delta_ref, up_grad_ref, down_grad_ref,
    out_acc, row_acc, act_ref, hid_ref,
):
    step = pl.program_id(0)
    count = rows_ref.shape[0]
    slope = math.sqrt(2.0 / math.pi)

    @pl.when(step == 0)
    def _():
        out_acc[...] = jnp.zeros_like(out_acc)
        row_acc[...] = jnp.zeros_like(row_acc)

    @pl.loop(0, count // SPAN)
    def _(block):
        rows = pl.ds(pl.multiple_of(block * SPAN, SPAN), SPAN)
        hidden = nn(rows_ref[rows, :], up_ref[0])
        square = hidden * hidden
        curve = jnp.tanh(slope * hidden * (1.0 + 0.044715 * square))
        half = 0.5 * (1.0 + curve)
        act = (hidden * half).astype(BF16)
        act_ref[rows, :] = act
        out_acc[rows, :] += nn(act, down_ref[0])
        act_delta = nt(delta_ref[rows, :], down_ref[0])
        grad = half + 0.5 * hidden * (1.0 - curve * curve) * (
            slope * (1.0 + (3 * 0.044715) * square)
        )
        hid = (grad * act_delta).astype(BF16)
        hid_ref[rows, :] = hid
        row_acc[rows, :] += nt(hid, up_ref[0])

    down_grad_ref[0] = tn(act_ref[...], delta_ref[...]).astype(BF16)
    up_grad_ref[0] = tn(rows_ref[...], hid_ref[...]).astype(BF16)

    @pl.when(step == pl.num_programs(0) - 1)
    def _():
        out_ref[...] = out_acc[...].astype(BF16)
        row_delta_ref[...] = row_acc[...].astype(BF16)


def experts(rows, delta, up, down):
    count, width = rows.shape
    chunks, _, hidden = up.shape
    flat = pl.BlockSpec((count, width), lambda c: (0, 0))
    up_block = pl.BlockSpec((1, width, hidden), lambda c: (c, 0, 0))
    down_block = pl.BlockSpec((1, hidden, width), lambda c: (c, 0, 0))
    return pl.pallas_call(
        experts_kernel,
        grid=(chunks,),
        out_shape=(
            jax.ShapeDtypeStruct((count, width), BF16),
            jax.ShapeDtypeStruct((count, width), BF16),
            jax.ShapeDtypeStruct(up.shape, BF16),
            jax.ShapeDtypeStruct(down.shape, BF16),
        ),
        in_specs=[flat, flat, up_block, down_block],
        out_specs=(flat, flat, up_block, down_block),
        scratch_shapes=[
            pltpu.VMEM((count, width), F32),
            pltpu.VMEM((count, width), F32),
            pltpu.VMEM((count, hidden), BF16),
            pltpu.VMEM((count, hidden), BF16),
        ],
        compiler_params=pltpu.CompilerParams(vmem_limit_bytes=VMEM_BYTES),
        cost_estimate=pl.CostEstimate(
            flops=12 * count * width * hidden * chunks,
            bytes_accessed=30 * 10**6,
            transcendentals=count * hidden * chunks,
        ),
        name="experts",
    )(rows, delta, up, down)


def on_device(
    layer_input,
    norm_gain,
    query_weight,
    key_weight,
    value_weight,
    output_weight,
    bias_table,
    mixing_gain,
    router_weight,
    up_weight,
    down_weight,
    expert_routes,
    cotangent,
):
    shard_count = lax.axis_size("shard")
    group_count = lax.axis_size("expert")
    shard = lax.axis_index("shard")
    group = lax.axis_index("expert")
    row_count, width = layer_input.shape
    experts_all = router_weight.shape[1]
    capacity = max(2, 4 * row_count // experts_all)
    local = output_weight.shape[0]

    x_full = lax.all_gather(layer_input, "shard", axis=0, tiled=True)
    qkv_weight = jnp.concatenate([query_weight, key_weight, value_weight], axis=1)
    x_full, early_cotangent, early_up, early_down, early_routes = lax.optimization_barrier(
        (x_full, cotangent, up_weight, down_weight, expert_routes)
    )
    up_all = lax.all_gather(early_up[0], "shard", axis=0, tiled=False)
    down_all = lax.all_gather(early_down[0], "shard", axis=0, tiled=False)
    upstream_all = lax.all_gather(early_cotangent, "expert", axis=0, tiled=False)
    routes_all = lax.all_gather(early_routes, "expert", axis=0, tiled=False)

    branch_part, normed_full, q, k, v, attended, lse = attend(
        bias_table, x_full, norm_gain, qkv_weight, output_weight
    )
    branch = lax.psum_scatter(branch_part, "shard", scatter_dimension=0, tiled=True)

    input_values = layer_input.astype(F32)
    residual = input_values + branch.astype(F32)
    mix_scale = lax.rsqrt(jnp.mean(residual * residual, axis=-1, keepdims=True) + 1e-06)
    mixed = residual * mix_scale * mixing_gain
    logits = jnp.dot(
        mixed, router_weight, precision=lax.Precision.HIGHEST, preferred_element_type=F32
    )
    route_match = expert_routes[:, :, None] == jnp.arange(experts_all, dtype=jnp.int32)
    route_hot = route_match.astype(F32)
    chosen = jnp.sum(logits[:, None, :] * route_hot, axis=-1)
    gate_probs = jax.nn.softmax(chosen, axis=-1)

    mixed_all = lax.all_gather(mixed.astype(BF16), "expert", axis=0, tiled=False)
    gates_all = lax.all_gather(gate_probs, "expert", axis=0, tiled=False)

    owned = routes_all == group
    gate_here = jnp.sum(jnp.where(owned, gates_all, 0.0), axis=-1)
    named = jnp.any(owned, axis=-1)
    slot = jnp.cumsum(named.astype(jnp.int32), axis=1) - 1
    slot = jnp.where(named, slot, -1)
    selector = (slot[:, :, None] == jnp.arange(capacity, dtype=jnp.int32)).astype(BF16)
    rows = jnp.einsum("gtc,gtd->gcd", selector, mixed_all, preferred_element_type=F32).astype(BF16)
    output_delta = (gate_here[:, :, None] * upstream_all.astype(F32)).astype(BF16)
    deltas = jnp.einsum(
        "gtc,gtd->gcd", selector, output_delta, preferred_element_type=F32
    ).astype(BF16)
    expert_out, row_delta, up_part, down_part = experts(
        rows.reshape(group_count * capacity, width),
        deltas.reshape(group_count * capacity, width),
        up_all,
        down_all,
    )
    expert_out = expert_out.reshape(group_count, capacity, width)
    row_delta = row_delta.reshape(group_count, capacity, width)
    rows_back = jnp.einsum(
        "gtc,gcd->gtd", selector, row_delta, preferred_element_type=F32
    ).astype(BF16)
    picked = jnp.einsum("gtc,gcd->gtd", selector, expert_out, preferred_element_type=F32)
    gate_delta_here = jnp.sum(upstream_all.astype(F32) * picked, axis=-1)
    share = (gate_here[:, :, None] * picked).astype(BF16)
    rows_sum = lax.psum_scatter(
        rows_back.reshape(group_count * row_count, width), "expert", scatter_dimension=0, tiled=True
    )
    gate_delta_all = lax.all_gather(gate_delta_here, "expert", axis=0, tiled=False)
    mixture = lax.psum_scatter(
        share.reshape(group_count * row_count, width), "expert", scatter_dimension=0, tiled=True
    )
    up_grad = lax.psum_scatter(up_part, "shard", scatter_dimension=0, tiled=True)
    down_grad = lax.psum_scatter(down_part, "shard", scatter_dimension=0, tiled=True)

    layer_output = (residual + mixture.astype(F32)).astype(BF16)
    upstream = cotangent.astype(F32)
    gate_delta_own = lax.dynamic_index_in_dim(gate_delta_all, group, 1, keepdims=False)
    gate_delta = jnp.sum(gate_delta_own.T[:, None, :] * route_hot, axis=-1)
    chosen_delta = gate_probs * (
        gate_delta - jnp.sum(gate_probs * gate_delta, axis=-1, keepdims=True)
    )
    logit_delta = jnp.sum(chosen_delta[:, :, None] * route_hot, axis=1)
    router_part = jnp.einsum("td,te->de", mixed, logit_delta, precision=lax.Precision.HIGHEST)
    mixed_delta = rows_sum.astype(F32) + jnp.einsum(
        "te,de->td", logit_delta, router_weight, precision=lax.Precision.HIGHEST
    )
    mix_scaled = mixed_delta * mixing_gain
    mixing_part = jnp.sum(mixed_delta * residual * mix_scale, axis=0)
    residual_delta = (
        upstream
        + mix_scale * mix_scaled
        - residual * mix_scale**3 * jnp.mean(mix_scaled * residual, axis=-1, keepdims=True)
    )
    branch_delta = lax.all_gather(residual_delta.astype(BF16), "shard", axis=0, tiled=True)
    parts, total, gain_part, table_part = attend_back(
        bias_table, x_full, qkv_weight, output_weight, q, k, v, lse, branch_delta
    )
    normed_delta = lax.psum_scatter(total, "shard", scatter_dimension=0, tiled=True).astype(F32)
    qkv_part = jnp.einsum("rd,rc->dc", normed_full, parts, preferred_element_type=F32)
    output_part = jnp.einsum("rc,rd->cd", attended, branch_delta, preferred_element_type=F32)

    norm_scale = lax.rsqrt(jnp.mean(input_values * input_values, axis=-1, keepdims=True) + 1e-06)
    norm_scaled = normed_delta * norm_gain
    input_delta = (
        residual_delta
        + norm_scale * norm_scaled
        - input_values
        * norm_scale**3
        * jnp.mean(norm_scaled * input_values, axis=-1, keepdims=True)
    )
    qkv_grad, output_grad = lax.psum(
        (qkv_part.astype(BF16), output_part.astype(BF16)), "expert"
    )
    table_hot = (jnp.arange(shard_count) == shard).astype(F32)
    table_spread = table_hot[:, None, None] * table_part[None]
    small = jnp.concatenate(
        [
            gain_part.reshape(-1),
            mixing_part,
            router_part.reshape(-1),
            table_spread.reshape(-1),
        ]
    )
    small = lax.psum(small, ("expert", "shard"))
    gain_grad = small[:width]
    mixing_grad = small[width : 2 * width]
    router_grad = small[2 * width : 2 * width + width * experts_all].reshape(width, experts_all)
    table_all = small[2 * width + width * experts_all :].reshape(table_spread.shape)
    table_grad = lax.dynamic_index_in_dim(table_all, shard, 0, keepdims=False)
    qkv_grad = qkv_grad.astype(F32)
    return (
        layer_output,
        input_delta.astype(BF16),
        gain_grad,
        qkv_grad[:, :local],
        qkv_grad[:, local : 2 * local],
        qkv_grad[:, 2 * local :],
        output_grad.astype(F32),
        table_grad,
        mixing_grad,
        router_grad,
        up_grad.astype(F32),
        down_grad.astype(F32),
    )


def solution(mesh):
    return jax.shard_map(
        on_device,
        mesh=mesh,
        in_specs=(
            P(("expert", "shard"), None),
            P(),
            P(None, "shard"),
            P(None, "shard"),
            P(None, "shard"),
            P("shard", None),
            P(None, "shard"),
            P(),
            P(),
            P("expert", None, "shard"),
            P("expert", "shard", None),
            P(("expert", "shard"), None),
            P(("expert", "shard"), None),
        ),
        out_specs=(
            P(("expert", "shard"), None),
            P(("expert", "shard"), None),
            P(),
            P(None, "shard"),
            P(None, "shard"),
            P(None, "shard"),
            P("shard", None),
            P(None, "shard"),
            P(),
            P(),
            P("expert", None, "shard"),
            P("expert", "shard", None),
        ),
        check_vma=False,
    )
```

```python
import math

import jax
import jax.numpy as jnp
from jax import lax
from jax.experimental import pallas as pl
from jax.experimental.pallas import tpu as pltpu
from jax.sharding import PartitionSpec as P

HEAD_DIM = 64
BUCKETS = 32
MAX_DIST = 128
TILE = 128
SPAN = 256
SCALE = HEAD_DIM ** (-0.5)
VMEM_BYTES = 56 * 1024 * 1024
F32 = jnp.float32
BF16 = jnp.bfloat16


def thresholds():
    halfway = BUCKETS // 2
    values = list(range(halfway + 1))
    for bucket in range(halfway + 1, BUCKETS):
        values.append(
            int(math.ceil(halfway * (MAX_DIST / halfway) ** ((bucket - halfway) / halfway)))
        )
    return values


STARTS = thresholds()


def nn(a, b):
    return lax.dot_general(a, b, (((1,), (0,)), ((), ())), preferred_element_type=F32)


def nt(a, b):
    return lax.dot_general(a, b, (((1,), (1,)), ((), ())), preferred_element_type=F32)


def tn(a, b):
    return lax.dot_general(a, b, (((0,), (0,)), ((), ())), preferred_element_type=F32)


def tile_distance():
    key = lax.broadcasted_iota(jnp.int32, (TILE, TILE), 0)
    query = lax.broadcasted_iota(jnp.int32, (TILE, TILE), 1)
    return query - key


def bias_tiles(table_ref, head):
    near = tile_distance()

    def chain(distance):
        value = jnp.full((TILE, TILE), table_ref[0, head], F32)
        for bucket in range(1, BUCKETS):
            value = jnp.where(distance >= STARTS[bucket], table_ref[bucket, head], value)
        return value

    diagonal = jnp.where(near >= 0, chain(near), -1e30)
    beside = chain(near + TILE)
    far = jnp.full((TILE, TILE), table_ref[BUCKETS - 1, head], F32)
    masked = jnp.full((TILE, TILE), -1e30, F32)
    return diagonal, beside, far, masked


def pick_tile(tiles, offset):
    if offset < 0:
        return tiles[3]
    return tiles[min(offset, 2)]


def bias_block(tiles, block):
    per = SPAN // TILE
    strips = []
    for key_tile in range(per * (block + 1)):
        strips.append(
            jnp.concatenate(
                [pick_tile(tiles, per * block + part - key_tile) for part in range(per)], axis=1
            )
        )
    return jnp.concatenate(strips, axis=0)


def attend_kernel(
    table_ref, x_ref, gain_ref, qkv_weight_ref, out_weight_ref,
    branch_ref, normed_ref, q_ref, k_ref, v_ref, att_ref, lse_ref,
):
    length = x_ref.shape[0]
    heads = q_ref.shape[0]
    local = heads * HEAD_DIM
    for block in range(length // SPAN):
        rows = slice(block * SPAN, (block + 1) * SPAN)
        x = x_ref[rows, :].astype(F32)
        norm_scale = lax.rsqrt(jnp.mean(x * x, axis=-1, keepdims=True) + 1e-06)
        normed = (x * norm_scale * gain_ref[...]).astype(BF16)
        normed_ref[rows, :] = normed
        qkv = nn(normed, qkv_weight_ref[...])
        for head in range(heads):
            cols = head * HEAD_DIM
            query = qkv[:, cols : cols + HEAD_DIM].astype(BF16)
            q_ref[head, rows, :] = (query.astype(F32) * SCALE).astype(BF16)
            k_ref[head, rows, :] = qkv[:, local + cols : local + cols + HEAD_DIM].astype(BF16)
            v_ref[head, rows, :] = qkv[:, 2 * local + cols : 2 * local + cols + HEAD_DIM].astype(
                BF16
            )
    lse_ref[...] = jnp.zeros_like(lse_ref)
    for head in range(heads):
        tiles = bias_tiles(table_ref, head)
        values_t = v_ref[head].astype(F32).T.astype(BF16)
        for block in range(length // SPAN):
            rows = slice(block * SPAN, (block + 1) * SPAN)
            reach = (block + 1) * SPAN
            scores = nt(k_ref[head, :reach, :], q_ref[head, rows, :]) + bias_block(tiles, block)
            maximum = jnp.max(scores, axis=0, keepdims=True)
            expo = jnp.exp(scores - maximum)
            totals = jnp.sum(expo, axis=0, keepdims=True)
            out_t = nn(values_t[:, :reach], expo.astype(BF16)) / totals
            att_ref[rows, head * HEAD_DIM : (head + 1) * HEAD_DIM] = out_t.T.astype(BF16)
            lse_ref[head : head + 1, rows] = maximum + jnp.log(totals)
    for block in range(length // SPAN):
        rows = slice(block * SPAN, (block + 1) * SPAN)
        branch_ref[rows, :] = nn(att_ref[rows, :], out_weight_ref[...]).astype(BF16)


def vmem_spec():
    return pl.BlockSpec(memory_space=pltpu.VMEM)


def attend(table, x_full, gain, qkv_weight, out_weight):
    length, width = x_full.shape
    local = out_weight.shape[0]
    heads = local // HEAD_DIM
    head_shape = jax.ShapeDtypeStruct((heads, length, HEAD_DIM), BF16)
    return pl.pallas_call(
        attend_kernel,
        out_shape=(
            jax.ShapeDtypeStruct((length, width), BF16),
            jax.ShapeDtypeStruct((length, width), BF16),
            head_shape,
            head_shape,
            head_shape,
            jax.ShapeDtypeStruct((length, local), BF16),
            jax.ShapeDtypeStruct((8, length), F32),
        ),
        in_specs=[pl.BlockSpec(memory_space=pltpu.SMEM)] + [vmem_spec()] * 4,
        out_specs=(vmem_spec(),) * 7,
        compiler_params=pltpu.CompilerParams(vmem_limit_bytes=VMEM_BYTES),
        cost_estimate=pl.CostEstimate(
            flops=12 * 10**9, bytes_accessed=8 * 10**6, transcendentals=2 * 10**6
        ),
        name="attend",
    )(table, x_full, gain.reshape(1, width), qkv_weight, out_weight)


def attend_back_kernel(
    table_ref, x_ref, qkv_weight_ref, out_weight_ref, q_ref, k_ref, v_ref, lse_ref, delta_ref,
    parts_ref, total_ref, gain_ref, table_grad_ref,
    att_delta_ref, key_ref, value_ref,
):
    length = x_ref.shape[0]
    heads = q_ref.shape[0]
    local = heads * HEAD_DIM
    blocks = length // SPAN
    per = SPAN // TILE
    near = tile_distance()
    for block in range(blocks):
        rows = slice(block * SPAN, (block + 1) * SPAN)
        att_delta = nt(delta_ref[rows, :], out_weight_ref[...])
        for head in range(heads):
            att_delta_ref[head, rows, :] = att_delta[
                :, head * HEAD_DIM : (head + 1) * HEAD_DIM
            ].astype(BF16)
    for head in range(heads):
        tiles = bias_tiles(table_ref, head)
        keys_t = k_ref[head].astype(F32).T.astype(BF16)
        sum_near = jnp.zeros((TILE, TILE), F32)
        sum_next = jnp.zeros((TILE, TILE), F32)
        sum_far = jnp.zeros((1, SPAN), F32)
        key_ref[...] = jnp.zeros_like(key_ref)
        value_ref[...] = jnp.zeros_like(value_ref)
        for block in range(blocks):
            rows = slice(block * SPAN, (block + 1) * SPAN)
            reach = (block + 1) * SPAN
            query = q_ref[head, rows, :]
            delta = att_delta_ref[head, rows, :]
            scores = nt(k_ref[head, :reach, :], query) + bias_block(tiles, block)
            weights = jnp.exp(scores - lse_ref[head : head + 1, rows])
            weight_delta = nt(v_ref[head, :reach, :], delta)
            centre = jnp.sum(weights * weight_delta, axis=0, keepdims=True)
            score_delta = (weights * (weight_delta - centre)).astype(BF16)
            value_ref[:reach, :] += nn(weights.astype(BF16), delta)
            key_ref[:reach, :] += nn(score_delta, query)
            query_t = nn(keys_t[:, :reach], score_delta) * SCALE
            parts_ref[rows, head * HEAD_DIM : (head + 1) * HEAD_DIM] = query_t.T.astype(BF16)
            rounded = score_delta.astype(F32)
            far_keys = max(0, (per * block - 1) * TILE)
            if far_keys:
                sum_far = sum_far + jnp.sum(rounded[:far_keys, :], axis=0, keepdims=True)
            for key_tile in range(far_keys // TILE, per * (block + 1)):
                for part in range(per):
                    offset = per * block + part - key_tile
                    if offset < 0:
                        continue
                    piece = rounded[
                        key_tile * TILE : (key_tile + 1) * TILE, part * TILE : (part + 1) * TILE
                    ]
                    if offset == 0:
                        sum_near = sum_near + piece
                    elif offset == 1:
                        sum_next = sum_next + piece
                    else:
                        total = jnp.sum(piece, axis=0, keepdims=True)
                        sum_far = sum_far + jnp.concatenate(
                            [total, jnp.zeros((1, SPAN - TILE), F32)], axis=1
                        )
        base = local + head * HEAD_DIM
        parts_ref[:, base : base + HEAD_DIM] = key_ref[...].astype(BF16)
        base = 2 * local + head * HEAD_DIM
        parts_ref[:, base : base + HEAD_DIM] = value_ref[...].astype(BF16)
        lines = []
        for bucket in range(BUCKETS):
            line = jnp.zeros((1, TILE), F32)
            for distance, sums in ((near, sum_near), (near + TILE, sum_next)):
                inside = distance >= STARTS[bucket]
                if bucket + 1 < BUCKETS:
                    inside = inside & (distance < STARTS[bucket + 1])
                line = line + jnp.sum(jnp.where(inside, sums, 0.0), axis=0, keepdims=True)
            if bucket == BUCKETS - 1:
                line = line + sum_far[:, :TILE] + sum_far[:, TILE:]
            lines.append(line)
        table_grad_ref[:, head : head + 1] = jnp.sum(
            jnp.concatenate(lines, axis=0), axis=1, keepdims=True
        )
    gain = jnp.zeros((1, x_ref.shape[1]), F32)
    for block in range(blocks):
        rows = slice(block * SPAN, (block + 1) * SPAN)
        total = nt(parts_ref[rows, :], qkv_weight_ref[...])
        x = x_ref[rows, :].astype(F32)
        norm_scale = lax.rsqrt(jnp.mean(x * x, axis=-1, keepdims=True) + 1e-06)
        gain = gain + jnp.sum(total * x * norm_scale, axis=0, keepdims=True)
        total_ref[rows, :] = total.astype(BF16)
    gain_ref[...] = gain


def attend_back(table, x_full, qkv_weight, out_weight, q, k, v, lse, delta):
    length, width = x_full.shape
    local = out_weight.shape[0]
    heads = local // HEAD_DIM
    return pl.pallas_call(
        attend_back_kernel,
        out_shape=(
            jax.ShapeDtypeStruct((length, 3 * local), BF16),
            jax.ShapeDtypeStruct((length, width), BF16),
            jax.ShapeDtypeStruct((1, width), F32),
            jax.ShapeDtypeStruct((BUCKETS, heads), F32),
        ),
        in_specs=[pl.BlockSpec(memory_space=pltpu.SMEM)] + [vmem_spec()] * 8,
        out_specs=(vmem_spec(),) * 4,
        scratch_shapes=[
            pltpu.VMEM((heads, length, HEAD_DIM), BF16),
            pltpu.VMEM((length, HEAD_DIM), F32),
            pltpu.VMEM((length, HEAD_DIM), F32),
        ],
        compiler_params=pltpu.CompilerParams(vmem_limit_bytes=VMEM_BYTES),
        cost_estimate=pl.CostEstimate(
            flops=24 * 10**9, bytes_accessed=12 * 10**6, transcendentals=2 * 10**6
        ),
        name="attend_back",
    )(table, x_full, qkv_weight, out_weight, q, k, v, lse, delta)


def experts_kernel(
    rows_ref, delta_ref, up_ref, down_ref,
    out_ref, row_delta_ref, up_grad_ref, down_grad_ref,
    out_acc, row_acc, act_ref, hid_ref,
):
    step = pl.program_id(0)
    count = rows_ref.shape[0]
    slope = math.sqrt(2.0 / math.pi)

    @pl.when(step == 0)
    def _():
        out_acc[...] = jnp.zeros_like(out_acc)
        row_acc[...] = jnp.zeros_like(row_acc)

    @pl.loop(0, count // SPAN)
    def _(block):
        rows = pl.ds(pl.multiple_of(block * SPAN, SPAN), SPAN)
        hidden = nn(rows_ref[rows, :], up_ref[0])
        square = hidden * hidden
        curve = jnp.tanh(slope * hidden * (1.0 + 0.044715 * square))
        half = 0.5 * (1.0 + curve)
        act = (hidden * half).astype(BF16)
        act_ref[rows, :] = act
        out_acc[rows, :] += nn(act, down_ref[0])
        act_delta = nt(delta_ref[rows, :], down_ref[0])
        grad = half + 0.5 * hidden * (1.0 - curve * curve) * (
            slope * (1.0 + (3 * 0.044715) * square)
        )
        hid = (grad * act_delta).astype(BF16)
        hid_ref[rows, :] = hid
        row_acc[rows, :] += nt(hid, up_ref[0])

    down_grad_ref[0] = tn(act_ref[...], delta_ref[...]).astype(BF16)
    up_grad_ref[0] = tn(rows_ref[...], hid_ref[...]).astype(BF16)

    @pl.when(step == pl.num_programs(0) - 1)
    def _():
        out_ref[...] = out_acc[...].astype(BF16)
        row_delta_ref[...] = row_acc[...].astype(BF16)


def experts(rows, delta, up, down):
    count, width = rows.shape
    chunks, _, hidden = up.shape
    flat = pl.BlockSpec((count, width), lambda c: (0, 0))
    up_block = pl.BlockSpec((1, width, hidden), lambda c: (c, 0, 0))
    down_block = pl.BlockSpec((1, hidden, width), lambda c: (c, 0, 0))
    return pl.pallas_call(
        experts_kernel,
        grid=(chunks,),
        out_shape=(
            jax.ShapeDtypeStruct((count, width), BF16),
            jax.ShapeDtypeStruct((count, width), BF16),
            jax.ShapeDtypeStruct(up.shape, BF16),
            jax.ShapeDtypeStruct(down.shape, BF16),
        ),
        in_specs=[flat, flat, up_block, down_block],
        out_specs=(flat, flat, up_block, down_block),
        scratch_shapes=[
            pltpu.VMEM((count, width), F32),
            pltpu.VMEM((count, width), F32),
            pltpu.VMEM((count, hidden), BF16),
            pltpu.VMEM((count, hidden), BF16),
        ],
        compiler_params=pltpu.CompilerParams(vmem_limit_bytes=VMEM_BYTES),
        cost_estimate=pl.CostEstimate(
            flops=12 * count * width * hidden * chunks,
            bytes_accessed=30 * 10**6,
            transcendentals=count * hidden * chunks,
        ),
        name="experts",
    )(rows, delta, up, down)


def on_device(
    layer_input,
    norm_gain,
    query_weight,
    key_weight,
    value_weight,
    output_weight,
    bias_table,
    mixing_gain,
    router_weight,
    up_weight,
    down_weight,
    expert_routes,
    cotangent,
):
    shard_count = lax.axis_size("shard")
    group_count = lax.axis_size("expert")
    shard = lax.axis_index("shard")
    row_count, width = layer_input.shape
    experts_all = router_weight.shape[1]
    capacity = max(2, 4 * row_count // experts_all)
    local = output_weight.shape[0]

    x_full = lax.all_gather(layer_input, "shard", axis=0, tiled=True)
    qkv_weight = jnp.concatenate([query_weight, key_weight, value_weight], axis=1)
    x_full, early_up, early_down = lax.optimization_barrier((x_full, up_weight, down_weight))
    up_all = lax.all_gather(early_up[0], "shard", axis=0, tiled=False)
    down_all = lax.all_gather(early_down[0], "shard", axis=0, tiled=False)

    branch_part, normed_full, q, k, v, attended, lse = attend(
        bias_table, x_full, norm_gain, qkv_weight, output_weight
    )
    branch = lax.psum_scatter(branch_part, "shard", scatter_dimension=0, tiled=True)

    input_values = layer_input.astype(F32)
    residual = input_values + branch.astype(F32)
    mix_scale = lax.rsqrt(jnp.mean(residual * residual, axis=-1, keepdims=True) + 1e-06)
    mixed = residual * mix_scale * mixing_gain
    logits = jnp.dot(
        mixed, router_weight, precision=lax.Precision.HIGHEST, preferred_element_type=F32
    )
    route_match = expert_routes[:, :, None] == jnp.arange(experts_all, dtype=jnp.int32)
    route_hot = route_match.astype(F32)
    chosen = jnp.sum(logits[:, None, :] * route_hot, axis=-1)
    gate_probs = jax.nn.softmax(chosen, axis=-1)

    upstream = cotangent.astype(F32)
    output_delta = (gate_probs[:, :, None] * upstream[:, None, :]).astype(BF16)
    flat_match = route_match.reshape(2 * row_count, experts_all).astype(jnp.int32)
    slot_index = jnp.sum(jnp.cumsum(flat_match, axis=0) * flat_match, axis=-1) - 1
    position = (expert_routes.reshape(-1) * capacity + slot_index).reshape(row_count, 2)
    selector = (position[:, :, None] == jnp.arange(experts_all * capacity, dtype=jnp.int32)).astype(
        BF16
    )

    def exchange(values):
        return lax.all_to_all(
            values.reshape(group_count, -1, values.shape[-1]),
            "expert",
            split_axis=0,
            concat_axis=0,
            tiled=True,
        ).reshape(values.shape)

    send_rows = jnp.einsum(
        "tkp,td->pd", selector, mixed.astype(BF16), preferred_element_type=F32
    ).astype(BF16)
    send_deltas = jnp.einsum(
        "tkp,tkd->pd", selector, output_delta, preferred_element_type=F32
    ).astype(BF16)
    rows = exchange(send_rows)
    deltas = exchange(send_deltas)
    expert_out, row_delta, up_part, down_part = experts(rows, deltas, up_all, down_all)
    product = jnp.sum(deltas.astype(F32) * expert_out.astype(F32), axis=-1, keepdims=True)
    coarse = product.astype(BF16)
    fine = (product - coarse.astype(F32)).astype(BF16)
    column = lax.broadcasted_iota(jnp.int32, (product.shape[0], TILE), 1)
    beside = jnp.where(column == 0, coarse, jnp.where(column == 1, fine, jnp.zeros_like(fine)))
    returned = exchange(jnp.concatenate([row_delta, beside], axis=1))
    returned, late_out = lax.optimization_barrier((returned, expert_out))
    combined = exchange(late_out)
    rows_sum = jnp.einsum(
        "tkp,pd->td", selector, returned[:, :width], preferred_element_type=F32
    )
    products = jnp.sum(
        jnp.einsum("tkp,pc->tkc", selector, returned[:, width:], preferred_element_type=F32),
        axis=-1,
    )
    up_grad = lax.psum_scatter(up_part, "shard", scatter_dimension=0, tiled=True)
    down_grad = lax.psum_scatter(down_part, "shard", scatter_dimension=0, tiled=True)

    picked = jnp.einsum("tkp,pd->tkd", selector, combined, preferred_element_type=F32)
    mixture = jnp.sum(gate_probs[:, :, None] * picked, axis=1)
    layer_output = (residual + mixture).astype(BF16)
    chosen_delta = products - gate_probs * jnp.sum(products, axis=-1, keepdims=True)
    logit_delta = jnp.sum(chosen_delta[:, :, None] * route_hot, axis=1)
    router_part = jnp.einsum("td,te->de", mixed, logit_delta, precision=lax.Precision.HIGHEST)
    mixed_delta = rows_sum + jnp.einsum(
        "te,de->td", logit_delta, router_weight, precision=lax.Precision.HIGHEST
    )
    mix_scaled = mixed_delta * mixing_gain
    mixing_part = jnp.sum(mixed_delta * residual * mix_scale, axis=0)
    residual_delta = (
        upstream
        + mix_scale * mix_scaled
        - residual * mix_scale**3 * jnp.mean(mix_scaled * residual, axis=-1, keepdims=True)
    )
    branch_delta = lax.all_gather(residual_delta.astype(BF16), "shard", axis=0, tiled=True)
    parts, total, gain_part, table_part = attend_back(
        bias_table, x_full, qkv_weight, output_weight, q, k, v, lse, branch_delta
    )
    normed_delta = lax.psum_scatter(total, "shard", scatter_dimension=0, tiled=True).astype(F32)
    qkv_part = jnp.einsum("rc,rd->cd", parts, normed_full, preferred_element_type=F32)
    output_part = jnp.einsum("rc,rd->cd", attended, branch_delta, preferred_element_type=F32)

    norm_scale = lax.rsqrt(jnp.mean(input_values * input_values, axis=-1, keepdims=True) + 1e-06)
    norm_scaled = normed_delta * norm_gain
    input_delta = (
        residual_delta
        + norm_scale * norm_scaled
        - input_values
        * norm_scale**3
        * jnp.mean(norm_scaled * input_values, axis=-1, keepdims=True)
    )
    dense = jnp.concatenate([qkv_part.astype(BF16), output_part.astype(BF16)], axis=0)
    dense = exchange(dense).reshape(group_count, dense.shape[0] // group_count, width)
    dense = jnp.sum(dense.astype(F32), axis=0).astype(BF16)
    dense = lax.all_gather(dense, "expert", axis=0, tiled=True)
    qkv_grad = dense[: 3 * local].T
    output_grad = dense[3 * local :]
    table_hot = (jnp.arange(shard_count) == shard).astype(F32)
    table_spread = table_hot[:, None, None] * table_part[None]
    small = jnp.concatenate(
        [
            gain_part.reshape(-1),
            mixing_part,
            router_part.reshape(-1),
            table_spread.reshape(-1),
        ]
    )
    small = lax.psum(small, ("expert", "shard"))
    gain_grad = small[:width]
    mixing_grad = small[width : 2 * width]
    router_grad = small[2 * width : 2 * width + width * experts_all].reshape(width, experts_all)
    table_all = small[2 * width + width * experts_all :].reshape(table_spread.shape)
    table_grad = lax.dynamic_index_in_dim(table_all, shard, 0, keepdims=False)
    qkv_grad = qkv_grad.astype(F32)
    return (
        layer_output,
        input_delta.astype(BF16),
        gain_grad,
        qkv_grad[:, :local],
        qkv_grad[:, local : 2 * local],
        qkv_grad[:, 2 * local :],
        output_grad.astype(F32),
        table_grad,
        mixing_grad,
        router_grad,
        up_grad.astype(F32),
        down_grad.astype(F32),
    )


def solution(mesh):
    return jax.shard_map(
        on_device,
        mesh=mesh,
        in_specs=(
            P(("expert", "shard"), None),
            P(),
            P(None, "shard"),
            P(None, "shard"),
            P(None, "shard"),
            P("shard", None),
            P(None, "shard"),
            P(),
            P(),
            P("expert", None, "shard"),
            P("expert", "shard", None),
            P(("expert", "shard"), None),
            P(("expert", "shard"), None),
        ),
        out_specs=(
            P(("expert", "shard"), None),
            P(("expert", "shard"), None),
            P(),
            P(None, "shard"),
            P(None, "shard"),
            P(None, "shard"),
            P("shard", None),
            P(None, "shard"),
            P(),
            P(),
            P("expert", None, "shard"),
            P("expert", "shard", None),
        ),
        check_vma=False,
    )
```
